32 devices in a mesh: row: 8 (over z, y), col: 4 (over x, core).
Axes of the slice: x: 2, y: 2, z: 4, core: 2. Of those that a mesh axis runs over, the one named last changes fastest.
Arguments:
- bands: float32 [13, 256, 512], P(None, 'row', 'col'), may hold values from -6 to 6
- kern_small: float32 [13, 5, 5], replicated, may hold values from -1.25 to 1.25
- kern_large: float32 [13, 9, 9], replicated, may hold values from -0.625 to 0.625
- mix_weight: float32 [39, 64], replicated, may hold values from -2.4 to 2.4
- node_ids: int32 [256, 512], P('row', 'col'), may hold values from 0 to 1
- labels: int32 [256, 512], P('row', 'col'), may hold values from 0 to 39
- edges: int32 [64, 256], replicated, may hold values from -7000 to 13104, as said below
Outputs:
- hist: float32 [64, 2, 40, 256], P('row', None, None, 'col')
The draws below stay inside these ranges and needn't reach their ends.
Inputs may be any that keep to these rules, and one draw needn't show every extreme that they name: `edges`: strictly increasing along the bins.
All inputs are finite; a program needn't handle non-finite values.
Results may differ from the reference program's by a relative error of at most 0.0003.
Values sent between devices are 32-bit elements; how exact they have to be, the bound alone decides.
A program may use at most 128 MiB of HBM per device.

```python
import jax
import jax.numpy as jnp
from jax import lax

BANDS = 13
FEAT = 64
BINS = 256
CLASSES = 40
NODES = 2
NH = 256
NW = 512


def draw_labels(key, part):
    key = jax.random.fold_in(key, 11)
    patch_key, noise_key, chooser_key = jax.random.split(key, 3)
    patches = jax.random.randint(patch_key, (NH // 8, NW // 8), 0, CLASSES)
    regional = jnp.repeat(jnp.repeat(patches, 8, axis=0), 8, axis=1)
    scattered = jax.random.randint(noise_key, (NH, NW), 0, CLASSES)
    chooser = jax.random.randint(chooser_key, (NH, NW), 0, 4)
    return jnp.where(chooser == 0, scattered, regional).astype(jnp.int32)


def draw_edges(key, part):
    key = jax.random.fold_in(key, 5)
    first_key, step_key, top_key, low_key = jax.random.split(key, 4)
    first_edge = jax.random.randint(first_key, (FEAT, 1), -7000, -5000)
    increments = jax.random.randint(step_key, (FEAT, BINS - 1), 8, 72)
    top_row = jax.random.randint(top_key, (), 0, FEAT)
    low_row = (top_row + 1 + jax.random.randint(low_key, (), 0, FEAT - 1)) % FEAT
    row_index = jnp.arange(FEAT, dtype=jnp.int32)[:, None]
    first_edge = jnp.where(row_index == top_row, -5001, first_edge)
    first_edge = jnp.where(row_index == low_row, -7000, first_edge)
    increments = jnp.where(row_index == top_row, 71, increments)
    rest = first_edge + jnp.cumsum(increments, axis=1)
    return jnp.concatenate([first_edge, rest], axis=1).astype(jnp.int32)


def plant(values, stream_key, least, largest):
    longest = values.shape.index(max(values.shape))
    spots = []
    for shift in (0, 1):
        where = [jax.random.randint(jax.random.fold_in(stream_key, axis), (), 0, length) for axis, length in enumerate(values.shape)]
        where[longest] = (where[longest] + shift) % values.shape[longest]
        spots.append(tuple(where))
    return values.at[spots[0]].set(least).at[spots[1]].set(largest)


def steps_of(rng, shape, shards, low, largest):
    level, own = 1.0, jax.random.fold_in(rng, 6)
    for dim, blocks in shards:
        heights = jnp.exp(jax.random.uniform(jax.random.fold_in(own, dim), (blocks,), jnp.float32, low / len(shards), largest / len(shards)))
        level = level * jnp.repeat(heights, shape[dim] // blocks).reshape([-1 if axis == dim else 1 for axis in range(len(shape))])
    return level


def scatter_about(own_key, extent, width, bound, cuts=(), held_as=jnp.bfloat16):
    drawn = jax.random.normal(own_key, extent, jnp.float32) * width
    if len(cuts) > 0:
        drawn = steps_of(own_key, extent, cuts, -0.22, 0.18) * drawn
    return jnp.clip(drawn, min=-bound, max=bound).astype(held_as)


def setup_inputs(seed: int = 0) -> dict:
    keys = jax.random.split(jax.random.key(seed), 8)
    bands = scatter_about(keys[0], (BANDS, NH, NW), 1.0, 6.0, ((1, 8), (2, 4)), jnp.float32)
    kern_small = scatter_about(keys[1], (BANDS, 5, 5), 25 ** -0.5, 1.25, (), jnp.float32)
    kern_large = scatter_about(keys[2], (BANDS, 9, 9), 81 ** -0.5, 0.625, (), jnp.float32)
    mix_weight = scatter_about(keys[3], (3 * BANDS, FEAT), 0.4, 2.4, (), jnp.float32)
    node_ids = plant(jax.random.randint(keys[4], (NH, NW), 0, NODES), jax.random.fold_in(keys[4], 1), 0, NODES - 1).astype(jnp.int32)
    labels = draw_labels(jax.random.fold_in(keys[7], 71), 0)
    edges = draw_edges(jax.random.fold_in(keys[7], 71), 0)
    return dict(bands=bands, kern_small=kern_small, kern_large=kern_large, mix_weight=mix_weight, node_ids=node_ids, labels=labels, edges=edges)


def stencil(padded, kernel, margin, tile_height, tile_width):
    reach = (kernel.shape[1] - 1) // 2
    running = jnp.zeros((padded.shape[0], tile_height, tile_width), jnp.float32)
    for row_off in range(kernel.shape[1]):
        for col_off in range(kernel.shape[2]):
            first_row = margin - reach + row_off
            first_col = margin - reach + col_off
            window = padded[:, first_row:first_row + tile_height, first_col:first_col + tile_width]
            running = running + kernel[:, row_off, col_off][:, None, None] * window
    return running


def reference(bands, kern_small, kern_large, mix_weight, node_ids, labels, edges):
    padded = jnp.pad(bands, ((0, 0), (4, 4), (4, 4)))
    small_field = stencil(padded, kern_small, 4, NH, NW)
    large_field = stencil(padded, kern_large, 4, NH, NW)
    stacked = jnp.concatenate([bands, small_field, large_field], axis=0).reshape(3 * BANDS, NH * NW)
    features_all = jnp.dot(mix_weight.T, stacked, precision=lax.Precision.HIGHEST, preferred_element_type=jnp.float32)
    centres_all = edges.astype(jnp.float32) / 1024.0
    cell_code = (node_ids.reshape(NH * NW) * CLASSES + labels.reshape(NH * NW)).astype(jnp.int32)

    def feature_hist(pair):
        values, centres = pair
        clamped = jnp.clip(values, centres[0], centres[BINS - 1])
        lower = jnp.clip(jnp.searchsorted(centres, clamped, side="right") - 1, 0, BINS - 2).astype(jnp.int32)
        bin_gaps = centres[1:] - centres[:-1]
        gap_here = bin_gaps[lower]
        lower_weight = jnp.clip((centres[lower + 1] - clamped) / gap_here, 0.0, 1.0).astype(jnp.bfloat16)
        upper_weight = jnp.clip((clamped - centres[lower]) / gap_here, 0.0, 1.0).astype(jnp.bfloat16)
        lower_weight, upper_weight = lax.optimization_barrier((lower_weight, upper_weight))
        weights = jnp.concatenate([lower_weight.astype(jnp.float32), upper_weight.astype(jnp.float32)])
        targets = jnp.concatenate([cell_code * BINS + lower, cell_code * BINS + lower + 1]).astype(jnp.int32)
        return jax.ops.segment_sum(weights, targets, num_segments=NODES * CLASSES * BINS)

    raw = lax.map(feature_hist, (features_all, centres_all))
    scale = float(NODES * CLASSES * BINS) / float(NH * NW)
    return raw.reshape(FEAT, NODES, CLASSES, BINS) * scale
```

```python
import functools

import jax
import jax.numpy as jnp
from jax import lax
from jax.experimental import pallas as pl
from jax.experimental.pallas import tpu as pltpu
from jax.sharding import PartitionSpec as P

FEAT = 64
BINS = 256
CLASSES = 40
NODES = 2
PAIRS = NODES * CLASSES
LANES = 128
MESH_ID = pl.DeviceIdType.MESH
VMEM = pl.BlockSpec(memory_space=pltpu.VMEM)
SMEM = pl.BlockSpec(memory_space=pltpu.SMEM)

DIRECTIONS = [(dr, dc) for dr in (-1, 0, 1) for dc in (-1, 0, 1) if (dr, dc) != (0, 0)]


def halo_kernel(rows, cols, bands_ref, out_ref, send_sem, recv_sem):
    height = bands_ref.shape[1]
    r = lax.axis_index("row")
    c = lax.axis_index("col")

    def inside(dr, dc):
        return (r + dr >= 0) & (r + dr < rows) & (c + dc >= 0) & (c + dc < cols)

    def row_span(d, far):
        if d == 0:
            return (0, height) if not far else (8, height)
        if d > 0:
            return (height - 8, 8) if not far else (0, 8)
        return (0, 8) if not far else (height + 8, 8)

    def copy_for(index):
        dr, dc = DIRECTIONS[index]
        from_row, count = row_span(dr, False)
        to_row, _ = row_span(dr, True)
        return pltpu.make_async_remote_copy(
            src_ref=bands_ref.at[:, pl.ds(from_row, count), :],
            dst_ref=out_ref.at[:, pl.ds(to_row, count), pl.ds((1 - dc) * LANES, LANES)],
            send_sem=send_sem.at[index],
            recv_sem=recv_sem.at[index],
            device_id=(r + dr, c + dc),
            device_id_type=MESH_ID,
        )

    barrier = pltpu.get_barrier_semaphore()
    depth = out_ref.shape[0]
    for dr, dc in DIRECTIONS:
        to_row, count = row_span(-dr, True)

        @pl.when(jnp.logical_not(inside(dr, dc)))
        def _():
            lane = (1 + dc) * LANES
            out_ref[:, to_row : to_row + count, lane : lane + LANES] = jnp.zeros(
                (depth, count, LANES), jnp.float32
            )

    for dr, dc in DIRECTIONS:

        @pl.when(inside(dr, dc))
        def _():
            pl.semaphore_signal(barrier, inc=1, device_id=(r + dr, c + dc), device_id_type=MESH_ID)

    tall = jnp.where(r > 0, 1, 0) + jnp.where(r < rows - 1, 1, 0) + 1
    wide = jnp.where(c > 0, 1, 0) + jnp.where(c < cols - 1, 1, 0) + 1
    pl.semaphore_wait(barrier, tall * wide - 1)

    for index, (dr, dc) in enumerate(DIRECTIONS):

        @pl.when(inside(dr, dc))
        def _():
            copy_for(index).start()

    out_ref[:, 8 : 8 + height, LANES : 2 * LANES] = bands_ref[...]
    for index, (dr, dc) in enumerate(DIRECTIONS):

        @pl.when(inside(dr, dc))
        def _():
            copy_for(index).wait_send()

        @pl.when(inside(-dr, -dc))
        def _():
            copy_for(index).wait_recv()


def exchange_halo(bands, rows, cols):
    depth, height, width = bands.shape
    return pl.pallas_call(
        functools.partial(halo_kernel, rows, cols),
        out_shape=jax.ShapeDtypeStruct((depth, height + 16, 3 * LANES), jnp.float32),
        in_specs=[VMEM],
        out_specs=VMEM,
        scratch_shapes=[pltpu.SemaphoreType.DMA((8,)), pltpu.SemaphoreType.DMA((8,))],
        compiler_params=pltpu.CompilerParams(
            collective_id=0, has_side_effects=True, vmem_limit_bytes=16 << 20
        ),
        name="halo",
    )(bands)


def feature_kernel(padded_ref, near_ref, far_ref, mix_ref, out_ref, shifted, stack):
    depth, tall, _ = padded_ref.shape
    height = tall - 16
    lane = lax.broadcasted_iota(jnp.int32, (height + 8, LANES), 1)

    def one_band(b, carry):
        left = padded_ref[b, 4 : 12 + height, 0:LANES]
        middle = padded_ref[b, 4 : 12 + height, LANES : 2 * LANES]
        right = padded_ref[b, 4 : 12 + height, 2 * LANES : 3 * LANES]
        for col_off in range(9):
            s = col_off - 4
            if s == 0:
                window = middle
            elif s > 0:
                window = pltpu.roll(jnp.where(lane >= s, middle, right), LANES - s, 1)
            else:
                window = pltpu.roll(jnp.where(lane < LANES + s, middle, left), -s, 1)
            shifted[col_off] = window
        small = jnp.zeros((height, LANES), jnp.float32)
        large = jnp.zeros((height, LANES), jnp.float32)
        for row_off in range(9):
            for col_off in range(9):
                window = shifted[col_off, row_off : row_off + height, :]
                large = large + far_ref[b, row_off * 9 + col_off] * window
                if 2 <= row_off <= 6 and 2 <= col_off <= 6:
                    small = small + near_ref[b, (row_off - 2) * 5 + col_off - 2] * window
        stack[b] = middle[4 : 4 + height, :]
        stack[depth + b] = small
        stack[2 * depth + b] = large
        return carry

    lax.fori_loop(0, depth, one_band, 0)
    for i in range(height):
        channels = stack[:, i, :]
        out_ref[:, i * LANES : (i + 1) * LANES] = jnp.dot(
            mix_ref[...],
            channels,
            precision=lax.Precision.HIGHEST,
            preferred_element_type=jnp.float32,
        )


def compute_features(padded, kern_small, kern_large, mix_rows):
    depth, tall, _ = padded.shape
    height = tall - 16
    return pl.pallas_call(
        feature_kernel,
        out_shape=jax.ShapeDtypeStruct((FEAT, height * LANES), jnp.float32),
        in_specs=[VMEM, SMEM, SMEM, VMEM],
        out_specs=VMEM,
        scratch_shapes=[
            pltpu.VMEM((9, height + 8, LANES), jnp.float32),
            pltpu.VMEM((3 * depth, height, LANES), jnp.float32),
        ],
        compiler_params=pltpu.CompilerParams(vmem_limit_bytes=24 << 20),
        name="features",
    )(padded, kern_small.reshape(depth, 25), kern_large.reshape(depth, 81), mix_rows)


def swap_kernel(inner, cols, feats_ref, code_ref, feats_out, code_out, send_sem, recv_sem, own_sem):
    r = lax.axis_index("row")
    c = lax.axis_index("col")
    base = r - lax.rem(r, inner)
    me = lax.rem(r, inner) * cols + c
    group = inner * cols

    def peer(step):
        other = lax.rem(me + step, group)
        return other, (base + other // cols, lax.rem(other, cols))

    barrier = pltpu.get_barrier_semaphore()
    for step in range(1, group):
        pl.semaphore_signal(barrier, inc=1, device_id=peer(step)[1], device_id_type=MESH_ID)
    pl.semaphore_wait(barrier, group - 1)
    own = pltpu.make_async_copy(feats_ref.at[me], feats_out.at[me], own_sem.at[0])
    own.start()
    own_code = pltpu.make_async_copy(code_ref, code_out.at[me], own_sem.at[1])
    own_code.start()
    copies = []
    for step in range(1, group):
        other, device = peer(step)
        copies.append(
            pltpu.make_async_remote_copy(
                src_ref=feats_ref.at[other],
                dst_ref=feats_out.at[me],
                send_sem=send_sem.at[0, step],
                recv_sem=recv_sem.at[0, step],
                device_id=device,
                device_id_type=MESH_ID,
            )
        )
        copies.append(
            pltpu.make_async_remote_copy(
                src_ref=code_ref,
                dst_ref=code_out.at[me],
                send_sem=send_sem.at[1, step],
                recv_sem=recv_sem.at[1, step],
                device_id=device,
                device_id_type=MESH_ID,
            )
        )
    for copy in copies:
        copy.start()
    own.wait()
    own_code.wait()
    for copy in copies:
        copy.wait()


def swap_features(feats, code, inner, cols):
    group = inner * cols
    share, pixels = feats.shape[0] // group, feats.shape[1]
    return pl.pallas_call(
        functools.partial(swap_kernel, inner, cols),
        out_shape=[
            jax.ShapeDtypeStruct((group, share, pixels), jnp.float32),
            jax.ShapeDtypeStruct((group,) + code.shape, jnp.int32),
        ],
        in_specs=[VMEM, VMEM],
        out_specs=[VMEM, VMEM],
        scratch_shapes=[
            pltpu.SemaphoreType.DMA((2, group)),
            pltpu.SemaphoreType.DMA((2, group)),
            pltpu.SemaphoreType.DMA((2,)),
        ],
        compiler_params=pltpu.CompilerParams(
            collective_id=1, has_side_effects=True, vmem_limit_bytes=16 << 20
        ),
        name="swap",
    )(feats.reshape(group, share, pixels), code)


CHUNK_ROWS = 8


def hist_kernel(feats_ref, code_ref, centres_ref, out_ref, even_pos, odd_pos, even_w, odd_w):
    sources, share, pixels = feats_ref.shape
    low_table = centres_ref[:, 0:LANES]
    high_table = centres_ref[:, LANES : 2 * LANES]
    first = jnp.broadcast_to(low_table[:, 0:1], (share, LANES))
    centre = jnp.broadcast_to(high_table[:, 0:1], (share, LANES))
    last = jnp.broadcast_to(high_table[:, LANES - 1 : LANES], (share, LANES))
    span = CHUNK_ROWS * LANES
    chunks = pixels // span
    bin_rows = lax.broadcasted_iota(jnp.int32, (LANES, LANES), 0).astype(jnp.float32)
    bin_rows = bin_rows.astype(jnp.bfloat16)
    pair_rows = lax.broadcasted_iota(jnp.int32, (PAIRS, LANES), 0)
    zero = jnp.zeros((LANES, LANES), jnp.bfloat16)
    out_ref[...] = jnp.zeros_like(out_ref)

    def spread(row):
        block = jnp.broadcast_to(row, (16, LANES)).astype(jnp.bfloat16)
        return jnp.concatenate([block] * (LANES // 16), axis=0)

    def one_chunk(step, carry):
        source = step // chunks
        start = pl.multiple_of(lax.rem(step, chunks) * span, span)
        row_start = lax.rem(step, chunks) * CHUNK_ROWS
        for i in range(CHUNK_ROWS):
            v = feats_ref[source, :, pl.ds(start + i * LANES, LANES)]
            v = jnp.minimum(jnp.maximum(v, first), last)
            upper_half = v >= centre
            below = jnp.where(upper_half, centre, first)
            above = jnp.where(upper_half, last, centre)
            pos = jnp.zeros((share, LANES), jnp.int32)
            for bit in (64, 32, 16, 8, 4, 2, 1):
                cand = pos + bit
                probe = jnp.where(
                    upper_half,
                    jnp.take_along_axis(high_table, cand, axis=1, mode="promise_in_bounds"),
                    jnp.take_along_axis(low_table, cand, axis=1, mode="promise_in_bounds"),
                )
                right = v >= probe
                if bit == 1:
                    right = right & (probe < last)
                pos = jnp.where(right, cand, pos)
                below = jnp.where(right, probe, below)
                above = jnp.where(right, above, probe)
            lower = jnp.where(upper_half, pos + LANES, pos)
            gap = above - below
            fall = jnp.minimum(jnp.maximum((above - v) / gap, 0.0), 1.0)
            rise = jnp.minimum(jnp.maximum((v - below) / gap, 0.0), 1.0)
            is_odd = (lower & 1) == 1
            half = lower >> 1
            at = slice(i * LANES, (i + 1) * LANES)
            odd_pos[:, at] = half.astype(jnp.float32)
            even_pos[:, at] = jnp.where(is_odd, half + 1, half).astype(jnp.float32)
            even_w[:, at] = jnp.where(is_odd, rise, fall)
            odd_w[:, at] = jnp.where(is_odd, fall, rise)
        hot = []
        for i in range(CHUNK_ROWS):
            code = jnp.broadcast_to(code_ref[source, pl.ds(row_start + i, 1), :], (PAIRS, LANES))
            hot.append(jnp.where(code == pair_rows, 1.0, 0.0).astype(jnp.bfloat16))
        hot = jnp.concatenate(hot, axis=1)
        for f in range(share):
            columns = []
            for i in range(CHUNK_ROWS):
                at = slice(i * LANES, (i + 1) * LANES)
                even = jnp.where(
                    bin_rows == spread(even_pos[f : f + 1, at]), spread(even_w[f : f + 1, at]), zero
                )
                odd = jnp.where(
                    bin_rows == spread(odd_pos[f : f + 1, at]), spread(odd_w[f : f + 1, at]), zero
                )
                columns.append(jnp.concatenate([even, odd], axis=0))
            tent = jnp.concatenate(columns, axis=1)
            out_ref[f] += lax.dot_general(
                hot, tent, (((1,), (1,)), ((), ())), preferred_element_type=jnp.float32
            )
        return carry

    lax.fori_loop(0, sources * chunks, one_chunk, 0)


def histograms(feats, code, centres):
    sources, share, pixels = feats.shape
    span = CHUNK_ROWS * LANES
    return pl.pallas_call(
        hist_kernel,
        out_shape=jax.ShapeDtypeStruct((share, PAIRS, BINS), jnp.float32),
        in_specs=[VMEM, VMEM, VMEM],
        out_specs=VMEM,
        scratch_shapes=[pltpu.VMEM((share, span), jnp.float32)] * 4,
        compiler_params=pltpu.CompilerParams(vmem_limit_bytes=32 << 20),
        name="histograms",
    )(feats, code, centres)


def reduce_kernel(outer, inner, cols, scale, hist_ref, out_ref, parts, packed, slabs, send_a, recv_a, send_b, recv_b):
    r = lax.axis_index("row")
    c = lax.axis_index("col")
    z = r // inner
    y = lax.rem(r, inner)

    def along_z(step):
        other = lax.rem(z + step, outer)
        return other, (other * inner + y, c)

    def along_c(step):
        other = lax.rem(c + step, cols)
        return other, (r, other)

    barrier = pltpu.get_barrier_semaphore()
    for step in range(1, outer):
        pl.semaphore_signal(barrier, inc=1, device_id=along_z(step)[1], device_id_type=MESH_ID)
    for step in range(1, cols):
        pl.semaphore_signal(barrier, inc=1, device_id=along_c(step)[1], device_id_type=MESH_ID)
    pl.semaphore_wait(barrier, outer + cols - 2)

    copies = []
    for step in range(1, outer):
        other, device = along_z(step)
        copies.append(
            pltpu.make_async_remote_copy(
                src_ref=hist_ref.at[other],
                dst_ref=parts.at[step],
                send_sem=send_a.at[step],
                recv_sem=recv_a.at[step],
                device_id=device,
                device_id_type=MESH_ID,
            )
        )
        copies[-1].start()
    for copy in copies:
        copy.wait()

    lane = lax.broadcasted_iota(jnp.int32, (8, LANES), 1)
    odd_lane = (lane & 1) == 1
    second = lane >= LANES // 2
    pick = (lane & (LANES // 2 - 1)) >> 1

    def gather(table, index):
        return jnp.take_along_axis(table, index, axis=1, mode="promise_in_bounds")

    def one_block(block, carry):
        row = pl.multiple_of(block * 8, 8)
        total = []
        for k in range(2):
            halves = []
            for side in range(2):
                at = pl.ds(side * LANES, LANES)
                value = hist_ref[z, k, pl.ds(row, 8), at]
                for step in range(1, outer):
                    value = value + parts[step, k, pl.ds(row, 8), at]
                halves.append(value * scale)
            total.append(halves)
        for dest in range(cols):
            index = pick + dest * (LANES // cols)
            by_k = [
                jnp.where(odd_lane, gather(total[k][1], index), gather(total[k][0], index))
                for k in range(2)
            ]
            packed[dest, pl.ds(row, 8), :] = jnp.where(second, by_k[1], by_k[0])
        return carry

    lax.fori_loop(0, PAIRS // 8, one_block, 0)

    copies = []
    for step in range(1, cols):
        other, device = along_c(step)
        copies.append(
            pltpu.make_async_remote_copy(
                src_ref=packed.at[other],
                dst_ref=slabs.at[c],
                send_sem=send_b.at[step],
                recv_sem=recv_b.at[step],
                device_id=device,
                device_id_type=MESH_ID,
            )
        )
        copies[-1].start()
    slabs[c] = packed[c]
    for copy in copies:
        copy.wait()
    for source in range(cols):
        out_ref[2 * source] = slabs[source, :, 0 : LANES // 2]
        out_ref[2 * source + 1] = slabs[source, :, LANES // 2 : LANES]


def reduce_histograms(hist, outer, inner, cols, scale):
    return pl.pallas_call(
        functools.partial(reduce_kernel, outer, inner, cols, scale),
        out_shape=jax.ShapeDtypeStruct((2 * cols, PAIRS, LANES // 2), jnp.float32),
        in_specs=[VMEM],
        out_specs=VMEM,
        scratch_shapes=[
            pltpu.VMEM((outer, 2, PAIRS, BINS), jnp.float32),
            pltpu.VMEM((cols, PAIRS, LANES), jnp.float32),
            pltpu.VMEM((cols, PAIRS, LANES), jnp.float32),
            pltpu.SemaphoreType.DMA((outer,)),
            pltpu.SemaphoreType.DMA((outer,)),
            pltpu.SemaphoreType.DMA((cols,)),
            pltpu.SemaphoreType.DMA((cols,)),
        ],
        compiler_params=pltpu.CompilerParams(
            collective_id=2, has_side_effects=True, vmem_limit_bytes=24 << 20
        ),
        name="reduce",
    )(hist.reshape(outer, 2, PAIRS, BINS))


def body(rows, cols, bands, kern_small, kern_large, mix_weight, node_ids, labels, edges):
    band_count, tile_height, tile_width = bands.shape
    pixels = tile_height * tile_width
    scale = float(NODES * CLASSES * BINS) / float(pixels * rows * cols)
    centres = edges.astype(jnp.float32) / 1024.0
    code = node_ids * CLASSES + labels
    padded = exchange_halo(bands, rows, cols)
    share = FEAT // rows
    inner = 2
    outer = rows // inner
    if rows % inner == 0 and share == 2 * cols and cols * (BINS // cols) == BINS and BINS // cols == 64:
        mix_rows = mix_weight.T.reshape(outer, inner, cols, 2, 3 * band_count)
        mix_rows = mix_rows.transpose(1, 2, 0, 3, 4).reshape(FEAT, 3 * band_count)
        own = centres.reshape(outer, inner, cols, 2, BINS)
        own = own[:, lax.axis_index("row") % inner, lax.axis_index("col")].reshape(2 * outer, BINS)
        feats = compute_features(padded, kern_small, kern_large, mix_rows)
        feats, code = swap_features(feats, code, inner, cols)
        hist = histograms(feats, code, own)
        summed = reduce_histograms(hist, outer, inner, cols, scale)
        return summed.reshape(share, NODES, CLASSES, BINS // cols)
    feats = compute_features(padded, kern_small, kern_large, mix_weight.T)
    hist = jnp.concatenate(
        [
            histograms(feats[None, i : i + 8], code[None], centres[i : i + 8])
            for i in range(0, FEAT, 8)
        ]
    )
    hist = hist.reshape(FEAT, PAIRS, 2, BINS // 2).swapaxes(2, 3)
    ordered = hist.reshape(rows, share, NODES, CLASSES, cols, BINS // cols)
    ordered = ordered.transpose(0, 4, 1, 2, 3, 5).reshape(
        rows * cols * share, NODES, CLASSES, BINS // cols
    )
    summed = lax.psum_scatter(ordered, ("row", "col"), scatter_dimension=0, tiled=True)
    return summed * scale


def solution(mesh):
    return jax.shard_map(
        functools.partial(body, mesh.shape["row"], mesh.shape["col"]),
        mesh=mesh,
        in_specs=(P(None, "row", "col"), P(), P(), P(), P("row", "col"), P("row", "col"), P()),
        out_specs=P("row", None, None, "col"),
        check_vma=False,
    )
```

```python
import functools

import jax
import jax.numpy as jnp
from jax import lax
from jax.experimental import pallas as pl
from jax.experimental.pallas import tpu as pltpu
from jax.sharding import PartitionSpec as P

FEAT = 64
BINS = 256
CLASSES = 40
NODES = 2
PAIRS = NODES * CLASSES
LANES = 128
MESH_ID = pl.DeviceIdType.MESH
VMEM = pl.BlockSpec(memory_space=pltpu.VMEM)
SMEM = pl.BlockSpec(memory_space=pltpu.SMEM)

DIRECTIONS = [(dr, dc) for dr in (-1, 0, 1) for dc in (-1, 0, 1) if (dr, dc) != (0, 0)]


def halo_kernel(rows, cols, bands_ref, out_ref, send_sem, recv_sem):
    height = bands_ref.shape[1]
    r = lax.axis_index("row")
    c = lax.axis_index("col")

    def inside(dr, dc):
        return (r + dr >= 0) & (r + dr < rows) & (c + dc >= 0) & (c + dc < cols)

    def row_span(d, far):
        if d == 0:
            return (0, height) if not far else (8, height)
        if d > 0:
            return (height - 8, 8) if not far else (0, 8)
        return (0, 8) if not far else (height + 8, 8)

    def copy_for(index):
        dr, dc = DIRECTIONS[index]
        from_row, count = row_span(dr, False)
        to_row, _ = row_span(dr, True)
        return pltpu.make_async_remote_copy(
            src_ref=bands_ref.at[:, pl.ds(from_row, count), :],
            dst_ref=out_ref.at[:, pl.ds(to_row, count), pl.ds((1 - dc) * LANES, LANES)],
            send_sem=send_sem.at[index],
            recv_sem=recv_sem.at[index],
            device_id=(r + dr, c + dc),
            device_id_type=MESH_ID,
        )

    barrier = pltpu.get_barrier_semaphore()
    depth = out_ref.shape[0]
    for dr, dc in DIRECTIONS:
        to_row, count = row_span(-dr, True)

        @pl.when(jnp.logical_not(inside(dr, dc)))
        def _():
            lane = (1 + dc) * LANES
            out_ref[:, to_row : to_row + count, lane : lane + LANES] = jnp.zeros(
                (depth, count, LANES), jnp.float32
            )

    for dr, dc in DIRECTIONS:

        @pl.when(inside(dr, dc))
        def _():
            pl.semaphore_signal(barrier, inc=1, device_id=(r + dr, c + dc), device_id_type=MESH_ID)

    tall = jnp.where(r > 0, 1, 0) + jnp.where(r < rows - 1, 1, 0) + 1
    wide = jnp.where(c > 0, 1, 0) + jnp.where(c < cols - 1, 1, 0) + 1
    pl.semaphore_wait(barrier, tall * wide - 1)

    for index, (dr, dc) in enumerate(DIRECTIONS):

        @pl.when(inside(dr, dc))
        def _():
            copy_for(index).start()

    out_ref[:, 8 : 8 + height, LANES : 2 * LANES] = bands_ref[...]
    for index, (dr, dc) in enumerate(DIRECTIONS):

        @pl.when(inside(dr, dc))
        def _():
            copy_for(index).wait_send()

        @pl.when(inside(-dr, -dc))
        def _():
            copy_for(index).wait_recv()


def exchange_halo(bands, rows, cols):
    depth, height, width = bands.shape
    return pl.pallas_call(
        functools.partial(halo_kernel, rows, cols),
        out_shape=jax.ShapeDtypeStruct((depth, height + 16, 3 * LANES), jnp.float32),
        in_specs=[VMEM],
        out_specs=VMEM,
        scratch_shapes=[pltpu.SemaphoreType.DMA((8,)), pltpu.SemaphoreType.DMA((8,))],
        compiler_params=pltpu.CompilerParams(
            collective_id=0, has_side_effects=True, vmem_limit_bytes=16 << 20
        ),
        name="halo",
    )(bands)


def feature_kernel(padded_ref, near_ref, far_ref, mix_ref, out_ref, shifted, stack):
    depth, tall, _ = padded_ref.shape
    height = tall - 16
    lane = lax.broadcasted_iota(jnp.int32, (height + 8, LANES), 1)

    def one_band(b, carry):
        left = padded_ref[b, 4 : 12 + height, 0:LANES]
        middle = padded_ref[b, 4 : 12 + height, LANES : 2 * LANES]
        right = padded_ref[b, 4 : 12 + height, 2 * LANES : 3 * LANES]
        for col_off in range(9):
            s = col_off - 4
            if s == 0:
                window = middle
            elif s > 0:
                window = pltpu.roll(jnp.where(lane >= s, middle, right), LANES - s, 1)
            else:
                window = pltpu.roll(jnp.where(lane < LANES + s, middle, left), -s, 1)
            shifted[col_off] = window
        small = jnp.zeros((height, LANES), jnp.float32)
        large = jnp.zeros((height, LANES), jnp.float32)
        for row_off in range(9):
            for col_off in range(9):
                window = shifted[col_off, row_off : row_off + height, :]
                large = large + far_ref[b, row_off * 9 + col_off] * window
                if 2 <= row_off <= 6 and 2 <= col_off <= 6:
                    small = small + near_ref[b, (row_off - 2) * 5 + col_off - 2] * window
        stack[b] = middle[4 : 4 + height, :]
        stack[depth + b] = small
        stack[2 * depth + b] = large
        return carry

    lax.fori_loop(0, depth, one_band, 0)
    for i in range(height):
        channels = stack[:, i, :]
        out_ref[:, i * LANES : (i + 1) * LANES] = jnp.dot(
            mix_ref[...],
            channels,
            precision=lax.Precision.HIGHEST,
            preferred_element_type=jnp.float32,
        )


def compute_features(padded, kern_small, kern_large, mix_rows):
    depth, tall, _ = padded.shape
    height = tall - 16
    return pl.pallas_call(
        feature_kernel,
        out_shape=jax.ShapeDtypeStruct((FEAT, height * LANES), jnp.float32),
        in_specs=[VMEM, SMEM, SMEM, VMEM],
        out_specs=VMEM,
        scratch_shapes=[
            pltpu.VMEM((9, height + 8, LANES), jnp.float32),
            pltpu.VMEM((3 * depth, height, LANES), jnp.float32),
        ],
        compiler_params=pltpu.CompilerParams(vmem_limit_bytes=24 << 20),
        name="features",
    )(padded, kern_small.reshape(depth, 25), kern_large.reshape(depth, 81), mix_rows)


def accumulate(feats, code_of, centres_ref, pos_ref, w_ref, hot_ref, acc_ref):
    share, pixels = feats.shape
    height = pixels // LANES
    even_table = centres_ref[:, 0:LANES]
    odd_table = centres_ref[:, LANES : 2 * LANES]

    def edge(table, i):
        return jnp.broadcast_to(table[:, i : i + 1], (share, LANES))

    first, last = edge(even_table, 0), edge(odd_table, LANES - 1)
    at64, at32, at96 = [edge(even_table, i) for i in (64, 32, 96)]
    at16, at48, at80, at112 = [edge(even_table, i) for i in (16, 48, 80, 112)]
    for i in range(height):
        at = slice(i * LANES, (i + 1) * LANES)
        v = jnp.minimum(jnp.maximum(feats[:, at], first), last)
        right1 = v >= at64
        probe = jnp.where(right1, at96, at32)
        below = jnp.where(right1, at64, first)
        above = jnp.where(right1, last, at64)
        pos = jnp.where(right1, 64, 0)
        right2 = v >= probe
        below = jnp.where(right2, probe, below)
        above = jnp.where(right2, above, probe)
        pos = jnp.where(right2, pos + 32, pos)
        probe = jnp.where(right1, jnp.where(right2, at112, at80), jnp.where(right2, at48, at16))
        right3 = v >= probe
        below = jnp.where(right3, probe, below)
        above = jnp.where(right3, above, probe)
        pos = jnp.where(right3, pos + 16, pos)
        for bit in (8, 4, 2, 1):
            cand = pos + bit
            probe = jnp.take_along_axis(even_table, cand, axis=1, mode="promise_in_bounds")
            right = v >= probe
            pos = jnp.where(right, cand, pos)
            below = jnp.where(right, probe, below)
            above = jnp.where(right, above, probe)
        probe = jnp.take_along_axis(odd_table, pos, axis=1, mode="promise_in_bounds")
        right = (v >= probe) & (probe < last)
        below = jnp.where(right, probe, below)
        above = jnp.where(right, above, probe)
        gap = above - below
        fall = jnp.minimum(jnp.maximum((above - v) / gap, 0.0), 1.0)
        rise = jnp.minimum(jnp.maximum((v - below) / gap, 0.0), 1.0)
        pos_ref[0, :, at] = jnp.where(right, pos + 1, pos).astype(jnp.float32)
        pos_ref[1, :, at] = pos.astype(jnp.float32)
        w_ref[0, :, at] = jnp.where(right, rise, fall)
        w_ref[1, :, at] = jnp.where(right, fall, rise)
    rows = lax.broadcasted_iota(jnp.int32, (LANES, LANES), 0)
    for i in range(height):
        code = jnp.broadcast_to(code_of(i), (LANES, LANES))
        hot_ref[:, i * LANES : (i + 1) * LANES] = jnp.where(code == rows, 1.0, 0.0).astype(
            jnp.bfloat16
        )
    bin_rows = rows.astype(jnp.float32).astype(jnp.bfloat16)
    zero = jnp.zeros((LANES, LANES), jnp.bfloat16)

    def spread(row):
        block = jnp.broadcast_to(row, (16, LANES)).astype(jnp.bfloat16)
        return jnp.concatenate([block] * (LANES // 16), axis=0)

    hot = hot_ref[...]
    for f in range(share):
        for side in range(2):
            tent = []
            for i in range(height):
                at = slice(i * LANES, (i + 1) * LANES)
                hit = bin_rows == spread(pos_ref[side, f : f + 1, at])
                tent.append(jnp.where(hit, spread(w_ref[side, f : f + 1, at]), zero))
            acc_ref[f, side] += lax.dot_general(
                jnp.concatenate(tent, axis=1),
                hot,
                (((1,), (1,)), ((), ())),
                preferred_element_type=jnp.float32,
            )


def write_histograms(acc_ref, out_ref):
    for f in range(out_ref.shape[0]):
        for side in range(2):
            out_ref[f, :, side * LANES : (side + 1) * LANES] = acc_ref[f, side].T[:PAIRS]


def hist_kernel(feats_ref, code_ref, centres_ref, out_ref, pos_ref, w_ref, hot_ref, acc_ref):
    acc_ref[...] = jnp.zeros_like(acc_ref)
    accumulate(
        feats_ref, lambda i: code_ref[i : i + 1, :], centres_ref, pos_ref, w_ref, hot_ref, acc_ref
    )
    write_histograms(acc_ref, out_ref)


def work_buffers(share, pixels):
    return [
        pltpu.VMEM((2, share, pixels), jnp.float32),
        pltpu.VMEM((2, share, pixels), jnp.float32),
        pltpu.VMEM((LANES, pixels), jnp.bfloat16),
        pltpu.VMEM((share, 2, LANES, LANES), jnp.float32),
    ]


def split_bins(centres):
    return jnp.concatenate([centres[:, 0::2], centres[:, 1::2]], axis=1)


def histograms(feats, code, centres):
    share, pixels = feats.shape
    return pl.pallas_call(
        hist_kernel,
        out_shape=jax.ShapeDtypeStruct((share, PAIRS, BINS), jnp.float32),
        in_specs=[VMEM, VMEM, VMEM],
        out_specs=VMEM,
        scratch_shapes=work_buffers(share, pixels),
        compiler_params=pltpu.CompilerParams(vmem_limit_bytes=40 << 20),
        name="histograms",
    )(feats, code, split_bins(centres))


def swap_kernel(
    feats_ref, code_ref, centres_ref, out_ref,
    got, got_code, pos_ref, w_ref, hot_ref, acc_ref, send_sem, recv_sem,
):
    r = lax.axis_index("row")
    c = lax.axis_index("col")
    y, x, core = lax.rem(r, 2), c // 2, lax.rem(c, 2)

    def peer(step):
        other_y = lax.rem(y + step // 4, 2)
        other_c = lax.rem(x + lax.rem(step // 2, 2), 2) * 2 + lax.rem(core + lax.rem(step, 2), 2)
        return other_y * 4 + other_c, (r - y + other_y, other_c)

    def copies(step):
        other, device = peer(step)
        return (
            pltpu.make_async_remote_copy(
                src_ref=feats_ref.at[other],
                dst_ref=got.at[step],
                send_sem=send_sem.at[0, step],
                recv_sem=recv_sem.at[0, step],
                device_id=device,
                device_id_type=MESH_ID,
            ),
            pltpu.make_async_remote_copy(
                src_ref=code_ref,
                dst_ref=got_code.at[step],
                send_sem=send_sem.at[1, step],
                recv_sem=recv_sem.at[1, step],
                device_id=device,
                device_id_type=MESH_ID,
            ),
        )

    barrier = pltpu.get_barrier_semaphore()
    for step in range(1, 8):
        pl.semaphore_signal(barrier, inc=1, device_id=peer(jnp.int32(step))[1], device_id_type=MESH_ID)
    pl.semaphore_wait(barrier, 7)
    for step in range(1, 8):
        for copy in copies(jnp.int32(step)):
            copy.start()
    got[0] = feats_ref[y * 4 + c]
    got_code[0] = code_ref[...]
    acc_ref[...] = jnp.zeros_like(acc_ref)

    def one_source(step, carry):
        @pl.when(step > 0)
        def _():
            for copy in copies(step):
                copy.wait_recv()

        accumulate(
            got.at[step],
            lambda i: got_code[step, i : i + 1, :],
            centres_ref, pos_ref, w_ref, hot_ref, acc_ref,
        )
        return carry

    lax.fori_loop(0, 8, one_source, 0)
    for step in range(1, 8):
        for copy in copies(jnp.int32(step)):
            copy.wait_send()
    write_histograms(acc_ref, out_ref)


def swap_histograms(feats, code, centres):
    share, pixels = feats.shape[0] // 8, feats.shape[1]
    return pl.pallas_call(
        swap_kernel,
        out_shape=jax.ShapeDtypeStruct((share, PAIRS, BINS), jnp.float32),
        in_specs=[VMEM, VMEM, VMEM],
        out_specs=VMEM,
        scratch_shapes=[
            pltpu.VMEM((8, share, pixels), jnp.float32),
            pltpu.VMEM((8,) + code.shape, jnp.int32),
            *work_buffers(share, pixels),
            pltpu.SemaphoreType.DMA((2, 8)),
            pltpu.SemaphoreType.DMA((2, 8)),
        ],
        compiler_params=pltpu.CompilerParams(
            collective_id=1, has_side_effects=True, vmem_limit_bytes=40 << 20
        ),
        name="swap_histograms",
    )(feats.reshape(8, share, pixels), code, split_bins(centres))


def reduce_kernel(outer, inner, cols, scale, hist_ref, out_ref, parts, packed, slabs, send_a, recv_a, send_b, recv_b):
    r = lax.axis_index("row")
    c = lax.axis_index("col")
    z = r // inner
    y = lax.rem(r, inner)

    def along_z(step):
        other = lax.rem(z + step, outer)
        return other, (other * inner + y, c)

    def along_c(step):
        other = lax.rem(c + step, cols)
        return other, (r, other)

    barrier = pltpu.get_barrier_semaphore()
    for step in range(1, outer):
        pl.semaphore_signal(barrier, inc=1, device_id=along_z(step)[1], device_id_type=MESH_ID)
    for step in range(1, cols):
        pl.semaphore_signal(barrier, inc=1, device_id=along_c(step)[1], device_id_type=MESH_ID)
    pl.semaphore_wait(barrier, outer + cols - 2)

    copies = []
    for step in range(1, outer):
        other, device = along_z(step)
        copies.append(
            pltpu.make_async_remote_copy(
                src_ref=hist_ref.at[other],
                dst_ref=parts.at[step],
                send_sem=send_a.at[step],
                recv_sem=recv_a.at[step],
                device_id=device,
                device_id_type=MESH_ID,
            )
        )
        copies[-1].start()
    for copy in copies:
        copy.wait()

    lane = lax.broadcasted_iota(jnp.int32, (8, LANES), 1)
    odd_lane = (lane & 1) == 1
    second = lane >= LANES // 2
    pick = (lane & (LANES // 2 - 1)) >> 1

    def gather(table, index):
        return jnp.take_along_axis(table, index, axis=1, mode="promise_in_bounds")

    def one_block(block, carry):
        row = pl.multiple_of(block * 8, 8)
        total = []
        for k in range(2):
            halves = []
            for side in range(2):
                at = pl.ds(side * LANES, LANES)
                value = hist_ref[z, k, pl.ds(row, 8), at]
                for step in range(1, outer):
                    value = value + parts[step, k, pl.ds(row, 8), at]
                halves.append(value * scale)
            total.append(halves)
        for dest in range(cols):
            index = pick + dest * (LANES // cols)
            by_k = [
                jnp.where(odd_lane, gather(total[k][1], index), gather(total[k][0], index))
                for k in range(2)
            ]
            packed[dest, pl.ds(row, 8), :] = jnp.where(second, by_k[1], by_k[0])
        return carry

    lax.fori_loop(0, PAIRS // 8, one_block, 0)

    copies = []
    for step in range(1, cols):
        other, device = along_c(step)
        copies.append(
            pltpu.make_async_remote_copy(
                src_ref=packed.at[other],
                dst_ref=slabs.at[c],
                send_sem=send_b.at[step],
                recv_sem=recv_b.at[step],
                device_id=device,
                device_id_type=MESH_ID,
            )
        )
        copies[-1].start()
    slabs[c] = packed[c]
    for copy in copies:
        copy.wait()
    for source in range(cols):
        out_ref[2 * source] = slabs[source, :, 0 : LANES // 2]
        out_ref[2 * source + 1] = slabs[source, :, LANES // 2 : LANES]


def reduce_histograms(hist, outer, inner, cols, scale):
    return pl.pallas_call(
        functools.partial(reduce_kernel, outer, inner, cols, scale),
        out_shape=jax.ShapeDtypeStruct((2 * cols, PAIRS, LANES // 2), jnp.float32),
        in_specs=[VMEM],
        out_specs=VMEM,
        scratch_shapes=[
            pltpu.VMEM((outer, 2, PAIRS, BINS), jnp.float32),
            pltpu.VMEM((cols, PAIRS, LANES), jnp.float32),
            pltpu.VMEM((cols, PAIRS, LANES), jnp.float32),
            pltpu.SemaphoreType.DMA((outer,)),
            pltpu.SemaphoreType.DMA((outer,)),
            pltpu.SemaphoreType.DMA((cols,)),
            pltpu.SemaphoreType.DMA((cols,)),
        ],
        compiler_params=pltpu.CompilerParams(
            collective_id=2, has_side_effects=True, vmem_limit_bytes=24 << 20
        ),
        name="reduce",
    )(hist.reshape(outer, 2, PAIRS, BINS))


def body(rows, cols, bands, kern_small, kern_large, mix_weight, node_ids, labels, edges):
    band_count, tile_height, tile_width = bands.shape
    pixels = tile_height * tile_width
    scale = float(NODES * CLASSES * BINS) / float(pixels * rows * cols)
    centres = edges.astype(jnp.float32) / 1024.0
    code = node_ids * CLASSES + labels
    padded = exchange_halo(bands, rows, cols)
    share = FEAT // rows
    inner = 2
    outer = rows // inner
    if rows % inner == 0 and cols == 4 and share == 8:
        mix_rows = mix_weight.T.reshape(outer, inner, cols, 2, 3 * band_count)
        mix_rows = mix_rows.transpose(1, 2, 0, 3, 4).reshape(FEAT, 3 * band_count)
        own = centres.reshape(outer, inner, cols, 2, BINS)
        own = own[:, lax.axis_index("row") % inner, lax.axis_index("col")].reshape(2 * outer, BINS)
        feats = compute_features(padded, kern_small, kern_large, mix_rows)
        hist = swap_histograms(feats, code, own)
        summed = reduce_histograms(hist, outer, inner, cols, scale)
        return summed.reshape(share, NODES, CLASSES, BINS // cols)
    feats = compute_features(padded, kern_small, kern_large, mix_weight.T)
    hist = jnp.concatenate(
        [
            histograms(feats[i : i + 8], code, centres[i : i + 8])
            for i in range(0, FEAT, 8)
        ]
    )
    hist = hist.reshape(FEAT, PAIRS, 2, BINS // 2).swapaxes(2, 3)
    ordered = hist.reshape(rows, share, NODES, CLASSES, cols, BINS // cols)
    ordered = ordered.transpose(0, 4, 1, 2, 3, 5).reshape(
        rows * cols * share, NODES, CLASSES, BINS // cols
    )
    summed = lax.psum_scatter(ordered, ("row", "col"), scatter_dimension=0, tiled=True)
    return summed * scale


def solution(mesh):
    return jax.shard_map(
        functools.partial(body, mesh.shape["row"], mesh.shape["col"]),
        mesh=mesh,
        in_specs=(P(None, "row", "col"), P(), P(), P(), P("row", "col"), P("row", "col"), P()),
        out_specs=P("row", None, None, "col"),
        check_vma=False,
    )
```

```python
import functools

import jax
import jax.numpy as jnp
from jax import lax
from jax.experimental import pallas as pl
from jax.experimental.pallas import tpu as pltpu
from jax.sharding import PartitionSpec as P

FEAT = 64
BINS = 256
CLASSES = 40
NODES = 2
PAIRS = NODES * CLASSES
LANES = 128
MESH_ID = pl.DeviceIdType.MESH
VMEM = pl.BlockSpec(memory_space=pltpu.VMEM)
SMEM = pl.BlockSpec(memory_space=pltpu.SMEM)

DIRECTIONS = [(dr, dc) for dr in (-1, 0, 1) for dc in (-1, 0, 1) if (dr, dc) != (0, 0)]


def halo_kernel(rows, cols, bands_ref, out_ref, send_sem, recv_sem):
    height = bands_ref.shape[1]
    r = lax.axis_index("row")
    c = lax.axis_index("col")

    def inside(dr, dc):
        return (r + dr >= 0) & (r + dr < rows) & (c + dc >= 0) & (c + dc < cols)

    def row_span(d, far):
        if d == 0:
            return (0, height) if not far else (8, height)
        if d > 0:
            return (height - 8, 8) if not far else (0, 8)
        return (0, 8) if not far else (height + 8, 8)

    def copy_for(index):
        dr, dc = DIRECTIONS[index]
        from_row, count = row_span(dr, False)
        to_row, _ = row_span(dr, True)
        return pltpu.make_async_remote_copy(
            src_ref=bands_ref.at[:, pl.ds(from_row, count), :],
            dst_ref=out_ref.at[:, pl.ds(to_row, count), pl.ds((1 - dc) * LANES, LANES)],
            send_sem=send_sem.at[index],
            recv_sem=recv_sem.at[index],
            device_id=(r + dr, c + dc),
            device_id_type=MESH_ID,
        )

    barrier = pltpu.get_barrier_semaphore()
    depth = out_ref.shape[0]
    for dr, dc in DIRECTIONS:
        to_row, count = row_span(-dr, True)

        @pl.when(jnp.logical_not(inside(dr, dc)))
        def _():
            lane = (1 + dc) * LANES
            out_ref[:, to_row : to_row + count, lane : lane + LANES] = jnp.zeros(
                (depth, count, LANES), jnp.float32
            )

    for dr, dc in DIRECTIONS:

        @pl.when(inside(dr, dc))
        def _():
            pl.semaphore_signal(barrier, inc=1, device_id=(r + dr, c + dc), device_id_type=MESH_ID)

    tall = jnp.where(r > 0, 1, 0) + jnp.where(r < rows - 1, 1, 0) + 1
    wide = jnp.where(c > 0, 1, 0) + jnp.where(c < cols - 1, 1, 0) + 1
    pl.semaphore_wait(barrier, tall * wide - 1)

    for index, (dr, dc) in enumerate(DIRECTIONS):

        @pl.when(inside(dr, dc))
        def _():
            copy_for(index).start()

    out_ref[:, 8 : 8 + height, LANES : 2 * LANES] = bands_ref[...]
    for index, (dr, dc) in enumerate(DIRECTIONS):

        @pl.when(inside(dr, dc))
        def _():
            copy_for(index).wait_send()

        @pl.when(inside(-dr, -dc))
        def _():
            copy_for(index).wait_recv()


def exchange_halo(bands, rows, cols):
    depth, height, width = bands.shape
    return pl.pallas_call(
        functools.partial(halo_kernel, rows, cols),
        out_shape=jax.ShapeDtypeStruct((depth, height + 16, 3 * LANES), jnp.float32),
        in_specs=[VMEM],
        out_specs=VMEM,
        scratch_shapes=[pltpu.SemaphoreType.DMA((8,)), pltpu.SemaphoreType.DMA((8,))],
        compiler_params=pltpu.CompilerParams(
            collective_id=0, has_side_effects=True, vmem_limit_bytes=16 << 20
        ),
        name="halo",
    )(bands)


def feature_kernel(padded_ref, near_ref, far_ref, mix_ref, out_ref, shifted, stack):
    depth, tall, _ = padded_ref.shape
    height = tall - 16
    lane = lax.broadcasted_iota(jnp.int32, (height + 8, LANES), 1)

    def one_band(b, carry):
        left = padded_ref[b, 4 : 12 + height, 0:LANES]
        middle = padded_ref[b, 4 : 12 + height, LANES : 2 * LANES]
        right = padded_ref[b, 4 : 12 + height, 2 * LANES : 3 * LANES]
        for col_off in range(9):
            s = col_off - 4
            if s == 0:
                window = middle
            elif s > 0:
                window = pltpu.roll(jnp.where(lane >= s, middle, right), LANES - s, 1)
            else:
                window = pltpu.roll(jnp.where(lane < LANES + s, middle, left), -s, 1)
            shifted[col_off] = window
        small = jnp.zeros((height, LANES), jnp.float32)
        large = jnp.zeros((height, LANES), jnp.float32)
        for row_off in range(9):
            for col_off in range(9):
                window = shifted[col_off, row_off : row_off + height, :]
                large = large + far_ref[b, row_off * 9 + col_off] * window
                if 2 <= row_off <= 6 and 2 <= col_off <= 6:
                    small = small + near_ref[b, (row_off - 2) * 5 + col_off - 2] * window
        stack[b] = middle[4 : 4 + height, :]
        stack[depth + b] = small
        stack[2 * depth + b] = large
        return carry

    lax.fori_loop(0, depth, one_band, 0)
    for i in range(height):
        channels = stack[:, i, :]
        out_ref[:, i * LANES : (i + 1) * LANES] = jnp.dot(
            mix_ref[...],
            channels,
            precision=lax.Precision.HIGHEST,
            preferred_element_type=jnp.float32,
        )


def compute_features(padded, kern_small, kern_large, mix_rows):
    depth, tall, _ = padded.shape
    height = tall - 16
    return pl.pallas_call(
        feature_kernel,
        out_shape=jax.ShapeDtypeStruct((FEAT, height * LANES), jnp.float32),
        in_specs=[VMEM, SMEM, SMEM, VMEM],
        out_specs=VMEM,
        scratch_shapes=[
            pltpu.VMEM((9, height + 8, LANES), jnp.float32),
            pltpu.VMEM((3 * depth, height, LANES), jnp.float32),
        ],
        compiler_params=pltpu.CompilerParams(vmem_limit_bytes=24 << 20),
        name="features",
    )(padded, kern_small.reshape(depth, 25), kern_large.reshape(depth, 81), mix_rows)


def locate(feats, code_of, centres_ref, pos_ref, w_ref, hot_ref):
    share, pixels = feats.shape
    height = pixels // LANES
    even_table = centres_ref[:, 0:LANES]
    odd_table = centres_ref[:, LANES : 2 * LANES]

    def edge(table, i):
        return jnp.broadcast_to(table[:, i : i + 1], (share, LANES))

    first, last = edge(even_table, 0), edge(odd_table, LANES - 1)
    at64, at32, at96 = [edge(even_table, i) for i in (64, 32, 96)]
    at16, at48, at80, at112 = [edge(even_table, i) for i in (16, 48, 80, 112)]
    for i in range(height):
        at = slice(i * LANES, (i + 1) * LANES)
        v = jnp.minimum(jnp.maximum(feats[:, at], first), last)
        right1 = v >= at64
        probe = jnp.where(right1, at96, at32)
        below = jnp.where(right1, at64, first)
        above = jnp.where(right1, last, at64)
        pos = jnp.where(right1, 64, 0)
        right2 = v >= probe
        below = jnp.where(right2, probe, below)
        above = jnp.where(right2, above, probe)
        pos = jnp.where(right2, pos + 32, pos)
        probe = jnp.where(right1, jnp.where(right2, at112, at80), jnp.where(right2, at48, at16))
        right3 = v >= probe
        below = jnp.where(right3, probe, below)
        above = jnp.where(right3, above, probe)
        pos = jnp.where(right3, pos + 16, pos)
        for bit in (8, 4, 2, 1):
            cand = pos + bit
            probe = jnp.take_along_axis(even_table, cand, axis=1, mode="promise_in_bounds")
            right = v >= probe
            pos = jnp.where(right, cand, pos)
            below = jnp.where(right, probe, below)
            above = jnp.where(right, above, probe)
        probe = jnp.take_along_axis(odd_table, pos, axis=1, mode="promise_in_bounds")
        right = (v >= probe) & (probe < last)
        below = jnp.where(right, probe, below)
        above = jnp.where(right, above, probe)
        gap = above - below
        fall = jnp.minimum(jnp.maximum((above - v) / gap, 0.0), 1.0)
        rise = jnp.minimum(jnp.maximum((v - below) / gap, 0.0), 1.0)
        pos_ref[0, :, at] = jnp.where(right, pos + 1, pos).astype(jnp.float32)
        pos_ref[1, :, at] = pos.astype(jnp.float32)
        w_ref[0, :, at] = jnp.where(right, rise, fall)
        w_ref[1, :, at] = jnp.where(right, fall, rise)
    rows = lax.broadcasted_iota(jnp.int32, (LANES, LANES), 0)
    for i in range(height):
        code = jnp.broadcast_to(code_of(i), (LANES, LANES))
        hot_ref[:, i * LANES : (i + 1) * LANES] = jnp.where(code == rows, 1.0, 0.0).astype(
            jnp.bfloat16
        )


def accumulate(features, pos_ref, w_ref, hot_ref, acc_ref):
    height = hot_ref.shape[1] // LANES
    rows = lax.broadcasted_iota(jnp.int32, (LANES, LANES), 0)
    bin_rows = rows.astype(jnp.float32).astype(jnp.bfloat16)
    zero = jnp.zeros((LANES, LANES), jnp.bfloat16)

    def spread(row):
        block = jnp.broadcast_to(row, (16, LANES)).astype(jnp.bfloat16)
        return jnp.concatenate([block] * (LANES // 16), axis=0)

    hot = hot_ref[...]
    for f in features:
        for side in range(2):
            tent = []
            for i in range(height):
                at = slice(i * LANES, (i + 1) * LANES)
                hit = bin_rows == spread(pos_ref[side, f : f + 1, at])
                tent.append(jnp.where(hit, spread(w_ref[side, f : f + 1, at]), zero))
            acc_ref[f, side] += lax.dot_general(
                jnp.concatenate(tent, axis=1),
                hot,
                (((1,), (1,)), ((), ())),
                preferred_element_type=jnp.float32,
            )


def write_histograms(acc_ref, out_ref):
    for f in range(out_ref.shape[0]):
        for side in range(2):
            out_ref[f, :, side * LANES : (side + 1) * LANES] = acc_ref[f, side].T[:PAIRS]


def hist_kernel(feats_ref, code_ref, centres_ref, out_ref, pos_ref, w_ref, hot_ref, acc_ref):
    acc_ref[...] = jnp.zeros_like(acc_ref)
    locate(feats_ref, lambda i: code_ref[i : i + 1, :], centres_ref, pos_ref, w_ref, hot_ref)
    accumulate(range(out_ref.shape[0]), pos_ref, w_ref, hot_ref, acc_ref)
    write_histograms(acc_ref, out_ref)


def work_buffers(share, pixels):
    return [
        pltpu.VMEM((2, share, pixels), jnp.float32),
        pltpu.VMEM((2, share, pixels), jnp.float32),
        pltpu.VMEM((LANES, pixels), jnp.bfloat16),
        pltpu.VMEM((share, 2, LANES, LANES), jnp.float32),
    ]


def split_bins(centres):
    return jnp.concatenate([centres[:, 0::2], centres[:, 1::2]], axis=1)


def histograms(feats, code, centres):
    share, pixels = feats.shape
    return pl.pallas_call(
        hist_kernel,
        out_shape=jax.ShapeDtypeStruct((share, PAIRS, BINS), jnp.float32),
        in_specs=[VMEM, VMEM, VMEM],
        out_specs=VMEM,
        scratch_shapes=work_buffers(share, pixels),
        compiler_params=pltpu.CompilerParams(vmem_limit_bytes=40 << 20),
        name="histograms",
    )(feats, code, split_bins(centres))


def swap_kernel(
    outer, cols, scale, feats_ref, code_ref, centres_ref, out_ref,
    got, got_code, pos_ref, w_ref, hot_ref, acc_ref, hist, parts, packed, slabs,
    send_sem, recv_sem, send_a, recv_a, send_b, recv_b,
):
    r = lax.axis_index("row")
    c = lax.axis_index("col")
    y, x, core = lax.rem(r, 2), c // 2, lax.rem(c, 2)

    def peer(step):
        other_y = lax.rem(y + step // 4, 2)
        other_c = lax.rem(x + lax.rem(step // 2, 2), 2) * 2 + lax.rem(core + lax.rem(step, 2), 2)
        return other_y * 4 + other_c, (r - y + other_y, other_c)

    def copies(step):
        other, device = peer(step)
        return (
            pltpu.make_async_remote_copy(
                src_ref=feats_ref.at[other],
                dst_ref=got.at[step],
                send_sem=send_sem.at[0, step],
                recv_sem=recv_sem.at[0, step],
                device_id=device,
                device_id_type=MESH_ID,
            ),
            pltpu.make_async_remote_copy(
                src_ref=code_ref,
                dst_ref=got_code.at[step],
                send_sem=send_sem.at[1, step],
                recv_sem=recv_sem.at[1, step],
                device_id=device,
                device_id_type=MESH_ID,
            ),
        )

    z = r // 2
    half, odd = z // 2, lax.rem(z, 2)

    def partial_copy(step):
        to_odd = lax.rem(odd + step, 2)
        if step < 2:
            slot, other = to_odd, (1 - half) * 2 + to_odd
        else:
            to_odd = 1 - odd
            slot, other = 2 + to_odd, half * 2 + to_odd
        return pltpu.make_async_remote_copy(
            src_ref=hist.at[slot],
            dst_ref=parts.at[step],
            send_sem=send_a.at[step],
            recv_sem=recv_a.at[step],
            device_id=(other * 2 + y, c),
            device_id_type=MESH_ID,
        )

    def along_c(step):
        other = lax.rem(c + step, cols)
        return other, (r, other)

    barrier = pltpu.get_barrier_semaphore()
    for step in range(1, 8):
        pl.semaphore_signal(barrier, inc=1, device_id=peer(jnp.int32(step))[1], device_id_type=MESH_ID)
    for step in range(1, outer):
        pl.semaphore_signal(
            barrier,
            inc=1,
            device_id=(lax.rem(z + step, outer) * 2 + y, c),
            device_id_type=MESH_ID,
        )
    pl.semaphore_wait(barrier, 7 + outer - 1)
    for step in range(1, 8):
        for copy in copies(jnp.int32(step)):
            copy.start()
    got[0] = feats_ref[y * 4 + c]
    got_code[0] = code_ref[...]
    acc_ref[...] = jnp.zeros_like(acc_ref)

    def first_half(step, carry):
        @pl.when(step > 0)
        def _():
            for copy in copies(step):
                copy.wait_recv()

        views = (pos_ref.at[step], w_ref.at[step], hot_ref.at[step])
        locate(got.at[step], lambda i: got_code[step, i : i + 1, :], centres_ref, *views)
        accumulate(range(4), *views, acc_ref)
        return carry

    def second_half(step, carry):
        accumulate(range(4, 8), pos_ref.at[step], w_ref.at[step], hot_ref.at[step], acc_ref)
        return carry

    def write(features):
        for f in features:
            for side in range(2):
                at = slice(side * LANES, (side + 1) * LANES)
                hist[f // 2, f % 2, :, at] = acc_ref[f, side].T[:PAIRS]

    lax.fori_loop(0, 8, first_half, 0)
    write(range(4))
    partials = [partial_copy(step) for step in range(3)]
    partials[0].start()
    partials[1].start()
    lax.fori_loop(0, 8, second_half, 0)
    write(range(4, 8))
    partials[2].start()
    for step in range(1, 8):
        for copy in copies(jnp.int32(step)):
            copy.wait_send()
    for copy in partials:
        copy.wait()

    lane = lax.broadcasted_iota(jnp.int32, (8, LANES), 1)
    odd_lane = (lane & 1) == 1
    second = lane >= LANES // 2
    pick = (lane & (LANES // 2 - 1)) >> 1

    def gather(table, index):
        return jnp.take_along_axis(table, index, axis=1, mode="promise_in_bounds")

    def one_block(block, carry):
        row = pl.multiple_of(block * 8, 8)
        total = []
        for k in range(2):
            halves = []
            for side in range(2):
                at = pl.ds(side * LANES, LANES)
                value = hist[2 + odd, k, pl.ds(row, 8), at]
                for step in range(3):
                    value = value + parts[step, k, pl.ds(row, 8), at]
                halves.append(value * scale)
            total.append(halves)
        for dest in range(cols):
            index = pick + dest * (LANES // cols)
            by_k = [
                jnp.where(odd_lane, gather(total[k][1], index), gather(total[k][0], index))
                for k in range(2)
            ]
            packed[dest, pl.ds(row, 8), :] = jnp.where(second, by_k[1], by_k[0])
        return carry

    lax.fori_loop(0, PAIRS // 8, one_block, 0)

    copies = []
    for step in range(1, cols):
        other, device = along_c(step)
        copies.append(
            pltpu.make_async_remote_copy(
                src_ref=packed.at[other],
                dst_ref=slabs.at[c],
                send_sem=send_b.at[step],
                recv_sem=recv_b.at[step],
                device_id=device,
                device_id_type=MESH_ID,
            )
        )
        copies[-1].start()
    slabs[c] = packed[c]
    for copy in copies:
        copy.wait()
    for source in range(cols):
        out_ref[2 * source] = slabs[source, :, 0 : LANES // 2]
        out_ref[2 * source + 1] = slabs[source, :, LANES // 2 : LANES]


def swap_histograms(feats, code, centres, outer, cols, scale):
    share, pixels = feats.shape[0] // 8, feats.shape[1]
    return pl.pallas_call(
        functools.partial(swap_kernel, outer, cols, scale),
        out_shape=jax.ShapeDtypeStruct((2 * cols, PAIRS, LANES // 2), jnp.float32),
        in_specs=[VMEM, VMEM, VMEM],
        out_specs=VMEM,
        scratch_shapes=[
            pltpu.VMEM((8, share, pixels), jnp.float32),
            pltpu.VMEM((8,) + code.shape, jnp.int32),
            pltpu.VMEM((8, 2, share, pixels), jnp.float32),
            pltpu.VMEM((8, 2, share, pixels), jnp.float32),
            pltpu.VMEM((8, LANES, pixels), jnp.bfloat16),
            pltpu.VMEM((share, 2, LANES, LANES), jnp.float32),
            pltpu.VMEM((outer, 2, PAIRS, BINS), jnp.float32),
            pltpu.VMEM((3, 2, PAIRS, BINS), jnp.float32),
            pltpu.VMEM((cols, PAIRS, LANES), jnp.float32),
            pltpu.VMEM((cols, PAIRS, LANES), jnp.float32),
            pltpu.SemaphoreType.DMA((2, 8)),
            pltpu.SemaphoreType.DMA((2, 8)),
            pltpu.SemaphoreType.DMA((3,)),
            pltpu.SemaphoreType.DMA((3,)),
            pltpu.SemaphoreType.DMA((cols,)),
            pltpu.SemaphoreType.DMA((cols,)),
        ],
        compiler_params=pltpu.CompilerParams(
            collective_id=1, has_side_effects=True, vmem_limit_bytes=48 << 20
        ),
        name="swap_histograms",
    )(feats.reshape(8, share, pixels), code, split_bins(centres))


def body(rows, cols, bands, kern_small, kern_large, mix_weight, node_ids, labels, edges):
    band_count, tile_height, tile_width = bands.shape
    pixels = tile_height * tile_width
    scale = float(NODES * CLASSES * BINS) / float(pixels * rows * cols)
    centres = edges.astype(jnp.float32) / 1024.0
    code = node_ids * CLASSES + labels
    padded = exchange_halo(bands, rows, cols)
    share = FEAT // rows
    inner = 2
    outer = rows // inner
    if rows == 8 and cols == 4 and share == 8:
        far_half = lax.axis_index("row") < rows // 2
        mix_rows = mix_weight.T.reshape(outer, inner, cols, 2, 3 * band_count)
        mix_rows = jnp.where(far_half, jnp.roll(mix_rows, 2, axis=0), mix_rows)
        mix_rows = mix_rows.transpose(1, 2, 0, 3, 4).reshape(FEAT, 3 * band_count)
        own = centres.reshape(outer, inner, cols, 2, BINS)
        own = jnp.where(far_half, jnp.roll(own, 2, axis=0), own)
        own = own[:, lax.axis_index("row") % inner, lax.axis_index("col")].reshape(2 * outer, BINS)
        feats = compute_features(padded, kern_small, kern_large, mix_rows)
        summed = swap_histograms(feats, code, own, outer, cols, scale)
        return summed.reshape(share, NODES, CLASSES, BINS // cols)
    feats = compute_features(padded, kern_small, kern_large, mix_weight.T)
    hist = jnp.concatenate(
        [
            histograms(feats[i : i + 8], code, centres[i : i + 8])
            for i in range(0, FEAT, 8)
        ]
    )
    hist = hist.reshape(FEAT, PAIRS, 2, BINS // 2).swapaxes(2, 3)
    ordered = hist.reshape(rows, share, NODES, CLASSES, cols, BINS // cols)
    ordered = ordered.transpose(0, 4, 1, 2, 3, 5).reshape(
        rows * cols * share, NODES, CLASSES, BINS // cols
    )
    summed = lax.psum_scatter(ordered, ("row", "col"), scatter_dimension=0, tiled=True)
    return summed * scale


def solution(mesh):
    return jax.shard_map(
        functools.partial(body, mesh.shape["row"], mesh.shape["col"]),
        mesh=mesh,
        in_specs=(P(None, "row", "col"), P(), P(), P(), P("row", "col"), P("row", "col"), P()),
        out_specs=P("row", None, None, "col"),
        check_vma=False,
    )
```
